32 devices in a mesh: groups: 2 (over y), seq: 8 (over z, x), batch: 2 (over core).
Axes of the slice: x: 2, y: 2, z: 4, core: 2. Of those that a mesh axis runs over, the one named last changes fastest.
Arguments:
- inputs: bfloat16 [4, 2048, 512], P(('groups', 'batch'), 'seq'), parts along dimension 0, may hold values from -6 to 6
- cotangent: bfloat16 [4, 2048, 512], P(('groups', 'batch'), 'seq'), parts along dimension 0, may hold values from -6 to 6
- kernel_one: bfloat16 [3, 512, 256], P(None, 'seq'), may hold values from -0.15625 to 0.15625
- mix_one: bfloat16 [256, 512], P(None, 'seq'), may hold values from -0.375 to 0.375
- kernel_two: bfloat16 [3, 512, 256], P(None, 'seq'), may hold values from -0.15625 to 0.15625
- mix_two: bfloat16 [256, 512], P(None, 'seq'), may hold values from -0.375 to 0.375
Outputs:
- grad_inputs: bfloat16 [4, 2048, 512], P(('groups', 'batch'), 'seq'), parts along dimension 0
- scaled_first_kernel_gradient: bfloat16 [6, 512, 256], P('groups', ('seq', 'batch')), parts along dimension 0
- grad_kernel_two: bfloat16 [6, 512, 256], P('groups'), parts along dimension 0
The draws below stay inside these ranges and needn't reach their ends.
There are 2 independent parts, one for each index of `groups`. The reference program is written for one: setup_inputs(seed, part) draws one part's arguments, and reference() takes and returns one part's arrays. A program takes and returns all parts, laid end to end along the dimension named above; an argument that names none is the same for every part. Nothing has to cross between parts.
All inputs are finite; a program needn't handle non-finite values.
Results may differ from the reference program's by a relative error of at most 0.014.
Values may be sent and summed in bfloat16 or wider, within the bound.
A program may use at most 64 MiB of HBM per device.

```python
import math
import jax
import jax.numpy as jnp
from jax import lax

C = 512
HID = 256
FIRST_SPACING = 38
SECOND_SPACING = 58
POSITIONS = 2048
SAMPLES = 2


def strengthened(drawn, own_key, source, target, shards_of, factor):
    def block_of(axis_at):
        return (jnp.arange(drawn.shape[axis_at]) // (drawn.shape[axis_at] // shards_of)).reshape((-1,) + (1,) * (drawn.ndim - 1 - axis_at))

    near = jax.random.permutation(own_key, shards_of)[block_of(target)]
    other_side = (block_of(target) + shards_of // 2) % shards_of
    return jnp.where((block_of(source) == near) | (block_of(source) == other_side), factor * drawn, drawn)


def block_levels(key, dims, cuts, smallest, top_value):
    level, own = 1.0, jax.random.fold_in(key, 6)
    for dim, blocks in cuts:
        heights = jnp.exp(jax.random.uniform(jax.random.fold_in(own, dim), (blocks,), jnp.float32, smallest / len(cuts), top_value / len(cuts)))
        level = level * jnp.repeat(heights, dims[dim] // blocks).reshape([-1 if axis == dim else 1 for axis in range(len(dims))])
    return level


def normal_values(own_key, dims, spread, reach, split=(), dtype=jnp.bfloat16):
    level = block_levels(own_key, dims, split, -0.22, 0.18) if split else 1.0
    values = jax.random.normal(own_key, dims, jnp.float32) * spread * level
    return jnp.minimum(jnp.maximum(values, -reach), reach).astype(dtype)


def bell_draw_with(own_key, dims, deviation, most, pieces, heavy, dtype=jnp.bfloat16):
    entries = deviation * jax.random.normal(own_key, dims, jnp.float32)
    if pieces:
        entries = entries * block_levels(own_key, dims, pieces, -0.22, 0.18)
    return jnp.clip(strengthened(entries, jax.random.fold_in(own_key, 3), *heavy), -most, most).astype(dtype)


def setup_inputs(seed: int = 0, part: int = 0) -> dict:
    key_of = jax.random.split(jax.random.key(seed), 7)
    own_keys = jax.random.split(jax.random.fold_in(key_of[6], part), 7)
    inputs = bell_draw_with(own_keys[0], (SAMPLES, POSITIONS, C), 1.0, 6.0, ((0, 2), (1, 8)), (1, 2, 8, 2.0))
    cotangent = normal_values(own_keys[1], (SAMPLES, POSITIONS, C), 1.0, 6.0, ((0, 2), (1, 8)))
    kernel_one = normal_values(key_of[2], (3, C, HID), (3 * C) ** -0.5, 0.15625, ((1, 8),))
    mix_one = normal_values(key_of[3], (HID, C), HID ** -0.5, 0.375, ((1, 8),))
    kernel_two = normal_values(key_of[4], (3, C, HID), (3 * C) ** -0.5, 0.15625, ((1, 8),))
    mix_two = normal_values(key_of[5], (HID, C), HID ** -0.5, 0.375, ((1, 8),))
    return {"inputs": inputs, "cotangent": cotangent, "kernel_one": kernel_one, "mix_one": mix_one, "kernel_two": kernel_two, "mix_two": mix_two}


def gelu_exact(v):
    return 0.5 * v * (1.0 + jax.scipy.special.erf(v / math.sqrt(2.0)))

def gelu_slope(v):
    cdf = 0.5 * (1.0 + jax.scipy.special.erf(v / math.sqrt(2.0)))
    return cdf + v * jnp.exp(-0.5 * v * v) / math.sqrt(2.0 * math.pi)

def shift_pos(arr, dist):
    if dist > 0:
        return jnp.pad(arr, ((0, 0), (dist, 0), (0, 0)))[:, :-dist]
    return jnp.pad(arr, ((0, 0), (0, -dist), (0, 0)))[:, -dist:]

def flat_dot(left, right):
    width = left.shape[-1]
    out = jnp.dot(left.reshape(-1, width), right, preferred_element_type=jnp.float32)
    return out.reshape(left.shape[0], left.shape[1], -1)

def flat_dot_nt(left, right):
    width = left.shape[-1]
    out = lax.dot_general(left.reshape(-1, width), right, (((1,), (1,)), ((), ())), preferred_element_type=jnp.float32)
    return out.reshape(left.shape[0], left.shape[1], -1)

def flat_dot_tn(left, right):
    return lax.dot_general(left.reshape(-1, left.shape[-1]), right.reshape(-1, right.shape[-1]), (((0,), (0,)), ((), ())), preferred_element_type=jnp.float32)

def forward_block(stream, kernel, mixer, dist):
    hidden = gelu_exact(stream.astype(jnp.float32)).astype(jnp.bfloat16)
    inner = flat_dot(shift_pos(hidden, dist), kernel[0]) + flat_dot(hidden, kernel[1]) + flat_dot(shift_pos(hidden, -dist), kernel[2])
    active = gelu_exact(inner).astype(jnp.bfloat16)
    result = (stream.astype(jnp.float32) + flat_dot(active, mixer)).astype(jnp.bfloat16)
    return (result, hidden, inner)

def backward_block(stream, hidden, inner, kernel, mixer, dist, grad_out):
    grad_inner = (flat_dot_nt(grad_out, mixer) * gelu_slope(inner)).astype(jnp.bfloat16)
    above = shift_pos(grad_inner, -dist)
    below = shift_pos(grad_inner, dist)
    partial_value = jnp.stack([flat_dot_tn(hidden, above), flat_dot_tn(hidden, grad_inner), flat_dot_tn(hidden, below)])
    back = flat_dot_nt(grad_inner, kernel[1]) + flat_dot_nt(above, kernel[0]) + flat_dot_nt(below, kernel[2])
    grad_in = (grad_out.astype(jnp.float32) + back * gelu_slope(stream.astype(jnp.float32))).astype(jnp.bfloat16)
    return (grad_in, partial_value)

def reference(inputs, cotangent, kernel_one, mix_one, kernel_two, mix_two):
    first_spacing_offset = FIRST_SPACING
    second_spacing_offset = SECOND_SPACING
    middle, hidden_one, inner_one = forward_block(inputs, kernel_one, mix_one, first_spacing_offset)
    unused, hidden_two, inner_two = forward_block(middle, kernel_two, mix_two, second_spacing_offset)
    grad_mid, partial_two = backward_block(middle, hidden_two, inner_two, kernel_two, mix_two, second_spacing_offset, cotangent)
    grad_in, partial_one = backward_block(inputs, hidden_one, inner_one, kernel_one, mix_one, first_spacing_offset, grad_mid)
    factor = float(SAMPLES * POSITIONS) ** (-0.5)
    return (grad_in, (partial_one * factor).astype(jnp.bfloat16), (partial_two * factor).astype(jnp.bfloat16))
```

```python
import functools
import math

import jax
import jax.numpy as jnp
from jax import lax
from jax.experimental import pallas as pl
from jax.experimental.pallas import tpu as pltpu
from jax.sharding import PartitionSpec as P

FIRST_SPACING = 38
SECOND_SPACING = 58


def padded_2(cells, sides, width):
    for axis, dim in sides:
        count = lax.axis_size(axis)
        ends = count - 1
        head = lax.slice_in_dim(cells, 0, width, axis=dim)
        tail = lax.slice_in_dim(cells, cells.shape[dim] - width, cells.shape[dim], axis=dim)
        cells = jnp.concatenate(
            [
                lax.ppermute(tail, axis, [(i, (i + 1) % count) for i in range(ends)]),
                cells,
                lax.ppermute(head, axis, [((i + 1) % count, i) for i in range(ends)]),
            ],
            axis=dim,
        )
    return cells


def gelu_exact(v):
    return 0.5 * v * (1.0 + jax.scipy.special.erf(v / math.sqrt(2.0)))


def gelu_slope(v):
    cdf = 0.5 * (1.0 + jax.scipy.special.erf(v / math.sqrt(2.0)))
    return cdf + v * jnp.exp(-0.5 * v * v) / math.sqrt(2.0 * math.pi)


def mat_nn(left, right):
    return jnp.dot(left, right, preferred_element_type=jnp.float32)


def mat_nt(left, right):
    return lax.dot_general(
        left, right, (((1,), (1,)), ((), ())), preferred_element_type=jnp.float32
    )


def mat_tn(left, right):
    return lax.dot_general(
        left, right, (((0,), (0,)), ((), ())), preferred_element_type=jnp.float32
    )


def inner_convolved(before, hidden, after, kernel):
    return mat_nn(before, kernel[0]) + mat_nn(hidden, kernel[1]) + mat_nn(after, kernel[2])


def block_back(stream, hidden, grad_inner, above, below, kernel, grad_out):
    partial_value = jnp.stack(
        [mat_tn(hidden, above), mat_tn(hidden, grad_inner), mat_tn(hidden, below)]
    )
    back = mat_nt(grad_inner, kernel[1]) + mat_nt(above, kernel[0]) + mat_nt(below, kernel[2])
    grad_in = (grad_out.astype(jnp.float32) + back * gelu_slope(stream.astype(jnp.float32))).astype(
        jnp.bfloat16
    )
    return (grad_in, partial_value)


def shards(inputs, cotangent, kernel_one, mix_one, kernel_two, mix_two):
    stream = inputs[0]
    grad_top = cotangent[0]
    length = stream.shape[0]
    first_spacing_offset = FIRST_SPACING
    second_spacing_offset = SECOND_SPACING
    kern_a, mixer_a, kern_b, mixer_b = (
        lax.all_gather(kernel_one, "seq", axis=1, tiled=True),
        lax.all_gather(mix_one, "seq", axis=1, tiled=True),
        lax.all_gather(kernel_two, "seq", axis=1, tiled=True),
        lax.all_gather(mix_two, "seq", axis=1, tiled=True),
    )
    hidden_one = gelu_exact(stream.astype(jnp.float32)).astype(jnp.bfloat16)
    padded = padded_2(hidden_one, (("seq", 0),), first_spacing_offset)
    inner_one = inner_convolved(
        padded[:length], hidden_one, padded[2 * first_spacing_offset :], kern_a
    )
    active_one = gelu_exact(inner_one).astype(jnp.bfloat16)
    middle = (stream.astype(jnp.float32) + mat_nn(active_one, mixer_a)).astype(jnp.bfloat16)
    hidden_two = gelu_exact(middle.astype(jnp.float32)).astype(jnp.bfloat16)
    padded_two = padded_2(hidden_two, (("seq", 0),), second_spacing_offset)
    inner_two = inner_convolved(
        padded_two[:length], hidden_two, padded_two[2 * second_spacing_offset :], kern_b
    )
    grad_inner_two = (mat_nt(grad_top, mixer_b) * gelu_slope(inner_two)).astype(jnp.bfloat16)
    grad_pad_two = padded_2(grad_inner_two, (("seq", 0),), second_spacing_offset)
    grad_mid, partial_two = block_back(
        middle,
        hidden_two,
        grad_inner_two,
        grad_pad_two[2 * second_spacing_offset :],
        grad_pad_two[:length],
        kern_b,
        grad_top,
    )
    factor = float(length * lax.axis_size("seq") * lax.axis_size("batch")) ** (-0.5)
    share_two = lax.psum_scatter(partial_two, ("seq", "batch"), scatter_dimension=1, tiled=True)
    result_two = lax.all_gather(
        (share_two * factor).astype(jnp.bfloat16), ("seq", "batch"), axis=1, tiled=True
    )
    grad_inner_one = (mat_nt(grad_mid, mixer_a) * gelu_slope(inner_one)).astype(jnp.bfloat16)
    padded_gradient_rows = padded_2(grad_inner_one, (("seq", 0),), first_spacing_offset)
    grad_in, partial_one = block_back(
        stream,
        hidden_one,
        grad_inner_one,
        padded_gradient_rows[2 * first_spacing_offset :],
        padded_gradient_rows[:length],
        kern_a,
        grad_mid,
    )
    share_one = lax.psum_scatter(partial_one, ("seq", "batch"), scatter_dimension=1, tiled=True)
    return (grad_in[None], (share_one * factor).astype(jnp.bfloat16), result_two)


HALO = 256
MARGIN_MID, MARGIN_TWO, MARGIN_ONE = 192, 128, 64
TILE = 128


def nn(left, right):
    return jnp.dot(left, right, preferred_element_type=jnp.float32)


def nt(left, right):
    return lax.dot_general(
        left, right, (((1,), (1,)), ((), ())), preferred_element_type=jnp.float32
    )


def tn(left, right):
    return lax.dot_general(
        left, right, (((0,), (0,)), ((), ())), preferred_element_type=jnp.float32
    )


def cdf_of(v):
    return 0.5 + 0.5 * lax.erf(v * (1.0 / math.sqrt(2.0)))


def slope_of(v, cdf):
    return cdf + v * jnp.exp(-0.5 * v * v) * (1.0 / math.sqrt(2.0 * math.pi))


def over_rows(start, stop, tile, body):
    def step(i, carry):
        body(pl.multiple_of(start + i * tile, math.gcd(start, tile) if start else tile))
        return carry

    lax.fori_loop(0, (stop - start) // tile, step, 0)


def fused_kernel(
    n, zs, factor,
    x_ref, c_ref, k1_ref, m1_ref, k2_ref, m2_ref,
    gin_ref, first_ref, second_ref,
    w, xf, cf, h1, s1, a0, a1, a2, u1, v1, x2, h2, s2, u2, du, cat, g1,
    pb, r1, sm, r2, q, r3, gb,
    wz_s, wz_r, wx_s, wx_r, wc_s, wc_r, hs, hr, p1s, p1r, p2s, p2r, p3s, p3r,
    gzs, gzr, gxs, gxr, gcs, gcr,
):
    bf, f32 = jnp.bfloat16, jnp.float32
    s = lax.axis_index("seq")
    b = lax.axis_index("batch")
    count = 2 * zs
    z, xx = s // 2, s % 2
    xp = s + 1 - 2 * xx
    rows = k1_ref.shape[1]
    sub = rows // 2

    def to(seq, batch):
        return {"seq": seq, "batch": batch}

    def copy(src, dst, send, recv, target):
        return pltpu.make_async_remote_copy(
            src_ref=src, dst_ref=dst, send_sem=send, recv_sem=recv,
            device_id=target, device_id_type=pl.DeviceIdType.MESH,
        )

    barrier = pltpu.get_barrier_semaphore()
    away = sorted({1, count - 1} | {2 * r for r in range(1, zs)})
    for d in away:
        pl.semaphore_signal(barrier, inc=1, device_id=to((s + d) % count, b), device_id_type=pl.DeviceIdType.MESH)
    pl.semaphore_signal(barrier, inc=1, device_id=to(s, 1 - b), device_id_type=pl.DeviceIdType.MESH)

    eye = (
        lax.broadcasted_iota(jnp.int32, (rows, rows), 0) == lax.broadcasted_iota(jnp.int32, (rows, rows), 1)
    ).astype(f32).astype(bf)
    for layer, (k_ref, m_ref) in enumerate(((k1_ref, m1_ref), (k2_ref, m2_ref))):
        for tap in range(3):
            w[layer, s, tap] = k_ref[tap]
        w[layer, s, 3] = nt(eye, m_ref[...]).astype(bf)
    pl.semaphore_wait(barrier, len(away) + 1)

    pending = []

    def launch(c):
        c.start()
        pending.append(c)
        return c

    halos = (
        (s < count - 1, s > 0, (s + 1) % count, n - HALO, 0, n - MARGIN_TWO, 0, 0),
        (s > 0, s < count - 1, (s + count - 1) % count, 0, HALO + n, 0, MARGIN_TWO + n, 2),
    )
    halo_copies = []
    for sends, receives, target, xsrc, xdst, csrc, cdst, at in halos:
        pair = (
            copy(x_ref.at[pl.ds(xsrc, HALO)], xf.at[pl.ds(xdst, HALO)], hs.at[at], hr.at[at], to(target, b)),
            copy(c_ref.at[pl.ds(csrc, MARGIN_TWO)], cf.at[pl.ds(cdst, MARGIN_TWO)], hs.at[at + 1], hr.at[at + 1], to(target, b)),
        )
        halo_copies.append((sends, receives, pair, xdst, cdst))

    def start_halo(which):
        for sends, receives, pair, xdst, cdst in halo_copies:
            @pl.when(sends)
            def _():
                pair[which].start()

    def half(layer, seq):
        return w.at[layer, seq, pl.ds(2 * b, 2)]

    def column(r, other=False):
        side = 1 - xx if other else xx
        return ((z + zs - r) % zs) * 2 + side

    wz, wx, wc = {}, {}, {}

    def send_x(layer, r):
        c = half(layer, column(r))
        wx[layer, r] = launch(copy(c, c, wx_s.at[layer, r], wx_r.at[layer, r], to(xp, b)))

    def send_core(layer, r, other):
        c = half(layer, column(r, other))
        at = r + (zs if other else 0)
        wc[layer, at] = launch(copy(c, c, wc_s.at[layer, at], wc_r.at[layer, at], to(s, 1 - b)))

    def weights_start(layer):
        for r in range(1, zs):
            c = half(layer, s)
            wz[layer, r] = launch(
                copy(c, c, wz_s.at[layer, r - 1], wz_r.at[layer, r - 1], to(((z + r) % zs) * 2 + xx, b))
            )
        send_x(layer, 0)

    def weights_z(layer):
        for r in [1, zs - 1] + list(range(2, zs - 1)):
            wz[layer, r].wait_recv()
            send_x(layer, r)
            send_core(layer, r, False)

    def weights_x(layer):
        for r in [0, 1, zs - 1] + list(range(2, zs - 1)):
            wx[layer, r].wait_recv()
            send_core(layer, r, True)

    def weights_core(layer):
        for at in range(1, 2 * zs):
            wc[layer, at].wait_recv()

    def tap_of(layer, tap):
        return w[layer, :, tap].reshape(count * rows, w.shape[-1])

    weights_start(0)
    start_halo(0)
    weights_start(1)
    start_halo(1)

    def own_gelu(t):
        v = x_ref[pl.ds(t, 16), :]
        xf[pl.ds(HALO + t, 16), :] = v
        v = v.astype(f32)
        cdf = cdf_of(v)
        h1[pl.ds(HALO + t, 16), :] = (v * cdf).astype(bf)
        s1[pl.ds(t, 16), :] = slope_of(v, cdf)

    over_rows(0, n, 16, own_gelu)
    cf[pl.ds(MARGIN_TWO, n), :] = c_ref[...]
    weights_z(0)

    for sends, receives, pair, xdst, cdst in halo_copies:
        @pl.when(receives)
        def _():
            pair[0].wait_recv()

        @pl.when(jnp.logical_not(receives))
        def _():
            xf[pl.ds(xdst, HALO), :] = jnp.zeros((HALO, xf.shape[1]), bf)

    def halo_gelu(t):
        v = xf[pl.ds(t, 16), :].astype(f32)
        h1[pl.ds(t, 16), :] = (v * cdf_of(v)).astype(bf)

    over_rows(0, HALO, 16, halo_gelu)
    weights_x(0)
    over_rows(HALO + n, 2 * HALO + n, 16, halo_gelu)
    weights_z(1)
    weights_core(0)

    def convolve(h, layer, total):
        def body(t):
            tile = h[pl.ds(t, TILE), :]
            a0[pl.ds(t, TILE), :] = nn(tile, tap_of(layer, 0))
            a1[pl.ds(t, TILE), :] = nn(tile, tap_of(layer, 1))
            a2[pl.ds(t, TILE), :] = nn(tile, tap_of(layer, 2))

        over_rows(0, total, TILE, body)

    mid = n + 2 * MARGIN_MID
    two = n + 2 * MARGIN_TWO
    one = n + 2 * MARGIN_ONE

    convolve(h1, 0, n + 2 * HALO)
    off = HALO - MARGIN_MID
    d = FIRST_SPACING
    for t in range(0, mid, 64):
        u1[pl.ds(t, 64), :] = (
            a0[pl.ds(t + off - d, 64), :] + a1[pl.ds(t + off, 64), :] + a2[pl.ds(t + off + d, 64), :]
        )

    def gelu_u1(t):
        v = u1[pl.ds(t, 32), :]
        v1[pl.ds(t, 32), :] = (v * cdf_of(v)).astype(bf)

    over_rows(0, mid, 32, gelu_u1)
    weights_x(1)

    def mix_body(t):
        out = xf[pl.ds(t + off, TILE), :].astype(f32) + nt(v1[pl.ds(t, TILE), :], tap_of(0, 3))
        x2[pl.ds(t, TILE), :] = out.astype(bf)

    over_rows(0, mid, TILE, mix_body)

    def gelu_x2(t):
        v = x2[pl.ds(t, 16), :].astype(f32)
        h2[pl.ds(t, 16), :] = (v * cdf_of(v)).astype(bf)

    lead = MARGIN_MID - MARGIN_ONE

    def both_x2(t):
        v = x2[pl.ds(t, 16), :].astype(f32)
        cdf = cdf_of(v)
        h2[pl.ds(t, 16), :] = (v * cdf).astype(bf)
        s2[pl.ds(t - lead, 16), :] = slope_of(v, cdf)

    over_rows(0, lead, 16, gelu_x2)
    over_rows(lead, lead + one, 16, both_x2)
    over_rows(lead + one, mid, 16, gelu_x2)

    @pl.when(s == 0)
    def _():
        h2[pl.ds(0, MARGIN_MID), :] = jnp.zeros((MARGIN_MID, h2.shape[1]), bf)

    @pl.when(s == count - 1)
    def _():
        h2[pl.ds(MARGIN_MID + n, MARGIN_MID), :] = jnp.zeros((MARGIN_MID, h2.shape[1]), bf)

    weights_core(1)
    convolve(h2, 1, mid)
    off2 = MARGIN_MID - MARGIN_TWO
    d = SECOND_SPACING
    for t in range(0, two, 64):
        u2[pl.ds(t, 64), :] = (
            a0[pl.ds(t + off2 - d, 64), :] + a1[pl.ds(t + off2, 64), :] + a2[pl.ds(t + off2 + d, 64), :]
        )

    for sends, receives, pair, xdst, cdst in halo_copies:
        @pl.when(receives)
        def _():
            pair[1].wait_recv()

        @pl.when(jnp.logical_not(receives))
        def _():
            cf[pl.ds(cdst, MARGIN_TWO), :] = jnp.zeros((MARGIN_TWO, cf.shape[1]), bf)

    def inner_two(t):
        v = u2[pl.ds(t, 64), :]
        du[pl.ds(t, 64), :] = nn(cf[pl.ds(t, 64), :], tap_of(1, 3)) * slope_of(v, cdf_of(v))

    over_rows(0, two, 64, inner_two)
    width = du.shape[1]

    def side_by_side(total, off, d):
        for t in range(0, total, 64):
            for k, at in enumerate((off + d, off, off - d)):
                cat[pl.ds(t, 64), pl.ds(k * width, width)] = du[pl.ds(t + at, 64), :].astype(bf)

    def partial(slot, h, first, offset):
        for k in range(3):
            p = tn(h[pl.ds(first, n), :], cat[pl.ds(offset, n), pl.ds(k * width, width)]).astype(bf)
            for i in range(2 * count):
                pb[slot, i % 2, (i // 2) % 2, i // 4, k] = p[i * sub : (i + 1) * sub]

    def reduce_core(slot):
        return launch(copy(pb.at[slot, 1 - b], r1.at[slot], p1s.at[slot], p1r.at[slot], to(s, 1 - b)))

    def reduce_x(slot, c):
        c.wait_recv()

        def add(side):
            for i in range(zs):
                sm[slot, side, i] = (
                    pb[slot, b, side, i].astype(f32) + r1[slot, side, i].astype(f32)
                ).astype(bf)

        add(1 - xx)
        c = launch(copy(sm.at[slot, 1 - xx], r2.at[slot], p2s.at[slot], p2r.at[slot], to(xp, b)))
        add(xx)
        return c

    def reduce_z(slot, c):
        c.wait_recv()
        for i in range(zs):
            q[slot, i] = (sm[slot, xx, i].astype(f32) + r2[slot, i].astype(f32)).astype(bf)
        return [
            launch(
                copy(
                    q.at[slot, (z + r) % zs], r3.at[slot, r - 1], p3s.at[slot, r - 1], p3r.at[slot, r - 1],
                    to(((z + r) % zs) * 2 + xx, b),
                )
            )
            for r in range(1, zs)
        ]

    def reduce_end(slot, cs):
        total = q[slot, z].astype(f32)
        for r, c in enumerate(cs):
            c.wait_recv()
            total += r3[slot, r].astype(f32)
        return (total * factor).astype(bf)

    side_by_side(one, MARGIN_TWO - MARGIN_ONE, SECOND_SPACING)
    partial(0, h2, MARGIN_MID, MARGIN_ONE)
    step_two = reduce_core(0)

    def back_of(t, layer, tile):
        out = nt(cat[pl.ds(t, tile), pl.ds(0, width)], tap_of(layer, 0))
        out += nt(cat[pl.ds(t, tile), pl.ds(width, width)], tap_of(layer, 1))
        return out + nt(cat[pl.ds(t, tile), pl.ds(2 * width, width)], tap_of(layer, 2))

    trim = MARGIN_TWO - MARGIN_ONE

    def grad_two(t):
        out = cf[pl.ds(t + trim, 64), :].astype(f32) + back_of(t, 1, 64) * s2[pl.ds(t, 64), :]
        g1[pl.ds(t, 64), :] = out.astype(bf)

    over_rows(0, one, 64, grad_two)

    @pl.when(s == 0)
    def _():
        g1[pl.ds(0, MARGIN_ONE), :] = jnp.zeros((MARGIN_ONE, g1.shape[1]), bf)

    @pl.when(s == count - 1)
    def _():
        g1[pl.ds(MARGIN_ONE + n, MARGIN_ONE), :] = jnp.zeros((MARGIN_ONE, g1.shape[1]), bf)

    step_two = reduce_x(0, step_two)

    def inner_one(t):
        v = u1[pl.ds(t + lead, 64), :]
        du[pl.ds(t, 64), :] = nn(g1[pl.ds(t, 64), :], tap_of(0, 3)) * slope_of(v, cdf_of(v))

    over_rows(0, one, 64, inner_one)
    side_by_side(n, MARGIN_ONE, FIRST_SPACING)
    partial(1, h1, HALO, 0)
    step_one = reduce_core(1)
    step_two = reduce_z(0, step_two)
    step_one = reduce_x(1, step_one)

    def grad_one(t):
        out = g1[pl.ds(t + MARGIN_ONE, 64), :].astype(f32) + back_of(t, 0, 64) * s1[pl.ds(t, 64), :]
        gin_ref[pl.ds(t, 64), :] = out.astype(bf)

    over_rows(0, n, 64, grad_one)

    gb[b, xx, z] = reduce_end(0, step_two)
    own = gb.at[b, xx, z]
    along_z = [
        launch(copy(own, own, gzs.at[r - 1], gzr.at[r - 1], to(((z + r) % zs) * 2 + xx, b)))
        for r in range(1, zs)
    ]
    step_one = reduce_z(1, step_one)
    for c in along_z:
        c.wait_recv()
    whole = gb.at[b, xx]
    along_x = launch(copy(whole, whole, gxs, gxr, to(xp, b)))
    first_ref[...] = reduce_end(1, step_one)
    along_x.wait_recv()
    whole = gb.at[b]
    launch(copy(whole, whole, gcs, gcr, to(s, 1 - b))).wait_recv()
    for i in range(2 * count):
        for k in range(3):
            second_ref[k, pl.ds(i * sub, sub), :] = gb[i % 2, (i // 2) % 2, i // 4, k]

    for c in pending:
        c.wait_send()
    for sends, receives, pair, xdst, cdst in halo_copies:
        @pl.when(sends)
        def _():
            pair[0].wait_send()
            pair[1].wait_send()


def fused(count, batch, inputs, cotangent, kernel_one, mix_one, kernel_two, mix_two):
    n, channels = inputs.shape[1:]
    _, rows, hid = kernel_one.shape
    sub = rows // 2
    zs = count // 2
    bf, f32 = jnp.bfloat16, jnp.float32
    mid, two, one, frame = n + 2 * MARGIN_MID, n + 2 * MARGIN_TWO, n + 2 * MARGIN_ONE, n + 2 * HALO
    vm = pltpu.VMEM
    dma = pltpu.SemaphoreType.DMA
    sems = []
    for shape in ((2, zs - 1), (2, zs), (2, 2 * zs), (4,), (2,), (2,), (2, zs - 1), (zs - 1,)):
        sems += [dma(shape), dma(shape)]
    sems += [dma, dma, dma, dma]
    grads = (3, sub, hid)
    spec = pl.BlockSpec(memory_space=pltpu.VMEM)
    gin, first, second = pl.pallas_call(
        functools.partial(fused_kernel, n, zs, float(n * count * batch) ** (-0.5)),
        out_shape=(
            jax.ShapeDtypeStruct((n, channels), bf),
            jax.ShapeDtypeStruct(grads, bf),
            jax.ShapeDtypeStruct((3, channels, hid), bf),
        ),
        in_specs=[spec] * 6,
        out_specs=(spec,) * 3,
        scratch_shapes=[
            vm((2, count, 4, rows, hid), bf),
            vm((frame, channels), bf),
            vm((two, channels), bf),
            vm((frame, channels), bf),
            vm((n, channels), f32),
            vm((frame, hid), f32),
            vm((frame, hid), f32),
            vm((frame, hid), f32),
            vm((mid, hid), f32),
            vm((mid, hid), bf),
            vm((mid, channels), bf),
            vm((mid, channels), bf),
            vm((one, channels), f32),
            vm((two, hid), f32),
            vm((two, hid), f32),
            vm((one, 3 * hid), bf),
            vm((one, channels), bf),
            vm((2, 2, 2, zs) + grads, bf),
            vm((2, 2, zs) + grads, bf),
            vm((2, 2, zs) + grads, bf),
            vm((2, zs) + grads, bf),
            vm((2, zs) + grads, bf),
            vm((2, zs - 1) + grads, bf),
            vm((2, 2, zs) + grads, bf),
        ]
        + sems,
        compiler_params=pltpu.CompilerParams(
            collective_id=0, has_side_effects=True, vmem_limit_bytes=52 * 2**20
        ),
    )(inputs[0], cotangent[0], kernel_one, mix_one, kernel_two, mix_two)
    return (gin[None], first, second)


def body(count, batch, inputs, *rest):
    n, rows = inputs.shape[1], rest[1].shape[1]
    fits = n >= HALO and n % TILE == 0 and rows % 32 == 0
    if fits and count % 2 == 0 and count >= 6 and batch == 2:
        return fused(count, batch, inputs, *rest)
    return shards(inputs, *rest)


def solution(mesh):
    placed = (
        P(("groups", "batch"), "seq", None),
        P(("groups", "batch"), "seq", None),
        P(None, "seq", None),
        P(None, "seq"),
        P(None, "seq", None),
        P(None, "seq"),
    )
    return jax.shard_map(
        functools.partial(body, mesh.shape["seq"], mesh.shape["batch"]),
        mesh=mesh,
        in_specs=placed,
        out_specs=(
            P(("groups", "batch"), "seq", None),
            P("groups", ("seq", "batch"), None),
            P("groups", None, None),
        ),
        check_vma=False,
    )
```

```python
import functools
import math

import jax
import jax.numpy as jnp
from jax import lax
from jax.experimental import pallas as pl
from jax.experimental.pallas import tpu as pltpu
from jax.sharding import PartitionSpec as P

FIRST_SPACING = 38
SECOND_SPACING = 58


def padded_2(cells, sides, width):
    for axis, dim in sides:
        count = lax.axis_size(axis)
        ends = count - 1
        head = lax.slice_in_dim(cells, 0, width, axis=dim)
        tail = lax.slice_in_dim(cells, cells.shape[dim] - width, cells.shape[dim], axis=dim)
        cells = jnp.concatenate(
            [
                lax.ppermute(tail, axis, [(i, (i + 1) % count) for i in range(ends)]),
                cells,
                lax.ppermute(head, axis, [((i + 1) % count, i) for i in range(ends)]),
            ],
            axis=dim,
        )
    return cells


def gelu_exact(v):
    return 0.5 * v * (1.0 + jax.scipy.special.erf(v / math.sqrt(2.0)))


def gelu_slope(v):
    cdf = 0.5 * (1.0 + jax.scipy.special.erf(v / math.sqrt(2.0)))
    return cdf + v * jnp.exp(-0.5 * v * v) / math.sqrt(2.0 * math.pi)


def mat_nn(left, right):
    return jnp.dot(left, right, preferred_element_type=jnp.float32)


def mat_nt(left, right):
    return lax.dot_general(
        left, right, (((1,), (1,)), ((), ())), preferred_element_type=jnp.float32
    )


def mat_tn(left, right):
    return lax.dot_general(
        left, right, (((0,), (0,)), ((), ())), preferred_element_type=jnp.float32
    )


def inner_convolved(before, hidden, after, kernel):
    return mat_nn(before, kernel[0]) + mat_nn(hidden, kernel[1]) + mat_nn(after, kernel[2])


def block_back(stream, hidden, grad_inner, above, below, kernel, grad_out):
    partial_value = jnp.stack(
        [mat_tn(hidden, above), mat_tn(hidden, grad_inner), mat_tn(hidden, below)]
    )
    back = mat_nt(grad_inner, kernel[1]) + mat_nt(above, kernel[0]) + mat_nt(below, kernel[2])
    grad_in = (grad_out.astype(jnp.float32) + back * gelu_slope(stream.astype(jnp.float32))).astype(
        jnp.bfloat16
    )
    return (grad_in, partial_value)


def shards(inputs, cotangent, kernel_one, mix_one, kernel_two, mix_two):
    stream = inputs[0]
    grad_top = cotangent[0]
    length = stream.shape[0]
    first_spacing_offset = FIRST_SPACING
    second_spacing_offset = SECOND_SPACING
    kern_a, mixer_a, kern_b, mixer_b = (
        lax.all_gather(kernel_one, "seq", axis=1, tiled=True),
        lax.all_gather(mix_one, "seq", axis=1, tiled=True),
        lax.all_gather(kernel_two, "seq", axis=1, tiled=True),
        lax.all_gather(mix_two, "seq", axis=1, tiled=True),
    )
    hidden_one = gelu_exact(stream.astype(jnp.float32)).astype(jnp.bfloat16)
    padded = padded_2(hidden_one, (("seq", 0),), first_spacing_offset)
    inner_one = inner_convolved(
        padded[:length], hidden_one, padded[2 * first_spacing_offset :], kern_a
    )
    active_one = gelu_exact(inner_one).astype(jnp.bfloat16)
    middle = (stream.astype(jnp.float32) + mat_nn(active_one, mixer_a)).astype(jnp.bfloat16)
    hidden_two = gelu_exact(middle.astype(jnp.float32)).astype(jnp.bfloat16)
    padded_two = padded_2(hidden_two, (("seq", 0),), second_spacing_offset)
    inner_two = inner_convolved(
        padded_two[:length], hidden_two, padded_two[2 * second_spacing_offset :], kern_b
    )
    grad_inner_two = (mat_nt(grad_top, mixer_b) * gelu_slope(inner_two)).astype(jnp.bfloat16)
    grad_pad_two = padded_2(grad_inner_two, (("seq", 0),), second_spacing_offset)
    grad_mid, partial_two = block_back(
        middle,
        hidden_two,
        grad_inner_two,
        grad_pad_two[2 * second_spacing_offset :],
        grad_pad_two[:length],
        kern_b,
        grad_top,
    )
    factor = float(length * lax.axis_size("seq") * lax.axis_size("batch")) ** (-0.5)
    share_two = lax.psum_scatter(partial_two, ("seq", "batch"), scatter_dimension=1, tiled=True)
    result_two = lax.all_gather(
        (share_two * factor).astype(jnp.bfloat16), ("seq", "batch"), axis=1, tiled=True
    )
    grad_inner_one = (mat_nt(grad_mid, mixer_a) * gelu_slope(inner_one)).astype(jnp.bfloat16)
    padded_gradient_rows = padded_2(grad_inner_one, (("seq", 0),), first_spacing_offset)
    grad_in, partial_one = block_back(
        stream,
        hidden_one,
        grad_inner_one,
        padded_gradient_rows[2 * first_spacing_offset :],
        padded_gradient_rows[:length],
        kern_a,
        grad_mid,
    )
    share_one = lax.psum_scatter(partial_one, ("seq", "batch"), scatter_dimension=1, tiled=True)
    return (grad_in[None], (share_one * factor).astype(jnp.bfloat16), result_two)


HALO, MARGIN_MID, MARGIN_ONE = 128, 64, 64
NEAR = 96
NEAR_TOP = 48
TILE = 128


def nn(left, right):
    return jnp.dot(left, right, preferred_element_type=jnp.float32)


def nt(left, right):
    return lax.dot_general(
        left, right, (((1,), (1,)), ((), ())), preferred_element_type=jnp.float32
    )


def tn(left, right):
    return lax.dot_general(
        left, right, (((0,), (0,)), ((), ())), preferred_element_type=jnp.float32
    )


def cdf_of(v):
    return 0.5 + 0.5 * lax.erf(v * (1.0 / math.sqrt(2.0)))


def slope_of(v, cdf):
    return cdf + v * jnp.exp(-0.5 * v * v) * (1.0 / math.sqrt(2.0 * math.pi))


def over_rows(start, stop, tile, body):
    def step(i, carry):
        body(pl.multiple_of(start + i * tile, math.gcd(start, tile) if start else tile))
        return carry

    lax.fori_loop(0, (stop - start) // tile, step, 0)


def fused_kernel(
    n, zs, factor,
    x_ref, c_ref, k1_ref, m1_ref, k2_ref, m2_ref,
    gin_ref, first_ref, second_ref,
    w, xf, cf, h1, s1, a0, a1, a2, u1, v1, x2, h2, s2, u2, du, cat, g1,
    pb, r1, sm, r2, q, r3, gb, db, dh,
    wz_s, wz_r, wx_s, wx_r, wc_s, wc_r, hs, hr, p1s, p1r, p2s, p2r, p3s, p3r,
    gzs, gzr, gxs, gxr, gcs, gcr, wy_s, wy_r, ds, dr,
):
    bf, f32 = jnp.bfloat16, jnp.float32
    s = lax.axis_index("seq")
    b = lax.axis_index("batch")
    g = lax.axis_index("groups")
    count = 2 * zs
    z, xx = s // 2, s % 2
    xp = s + 1 - 2 * xx
    rows = k1_ref.shape[1]
    sub = rows // 2

    def to(seq, batch):
        return {"seq": seq, "batch": batch}

    over_y = {"groups": 1 - g}

    def copy(src, dst, send, recv, target):
        return pltpu.make_async_remote_copy(
            src_ref=src, dst_ref=dst, send_sem=send, recv_sem=recv,
            device_id=target, device_id_type=pl.DeviceIdType.MESH,
        )

    barrier = pltpu.get_barrier_semaphore()
    away = sorted({1, count - 1} | {2 * r for r in range(1, zs)})
    for d in away:
        pl.semaphore_signal(barrier, inc=1, device_id=to((s + d) % count, b), device_id_type=pl.DeviceIdType.MESH)
    pl.semaphore_signal(barrier, inc=1, device_id=to(s, 1 - b), device_id_type=pl.DeviceIdType.MESH)

    pl.semaphore_signal(barrier, inc=1, device_id=over_y, device_id_type=pl.DeviceIdType.MESH)

    eye = (
        lax.broadcasted_iota(jnp.int32, (rows, rows), 0) == lax.broadcasted_iota(jnp.int32, (rows, rows), 1)
    ).astype(f32).astype(bf)
    for layer, (k_ref, m_ref) in enumerate(((k1_ref, m1_ref), (k2_ref, m2_ref))):
        for tap in range(3):
            w[layer, s, tap] = k_ref[tap]
        w[layer, s, 3] = nt(eye, m_ref[...]).astype(bf)
    pl.semaphore_wait(barrier, len(away) + 2)

    pending = []

    def launch(c):
        c.start()
        pending.append(c)
        return c

    halos = (
        (s < count - 1, s > 0, (s + 1) % count, 0),
        (s > 0, s < count - 1, (s + count - 1) % count, 1),
    )

    def edge(which, height, near):
        return (n - near, height - near) if which == 0 else (0, height + n)

    halo_copies = []
    for sends, receives, target, at in halos:
        xsrc, xdst = edge(at, HALO, NEAR)
        csrc, cdst = edge(at, MARGIN_ONE, NEAR_TOP)
        pair = (
            copy(x_ref.at[pl.ds(xsrc, NEAR)], xf.at[pl.ds(xdst, NEAR)], hs.at[2 * at], hr.at[2 * at], to(target, b)),
            copy(c_ref.at[pl.ds(csrc, NEAR_TOP)], cf.at[pl.ds(cdst, NEAR_TOP)], hs.at[2 * at + 1], hr.at[2 * at + 1], to(target, b)),
            copy(db.at[pl.ds(xsrc, NEAR)], dh.at[at], ds.at[at], dr.at[at], to(target, b)),
        )
        halo_copies.append((sends, receives, pair, xdst, cdst))

    def start_halo(which):
        for sends, receives, pair, xdst, cdst in halo_copies:
            @pl.when(sends)
            def _():
                pair[which].start()

    def quarter(layer, seq):
        return w.at[layer, seq, 2 * b + g]

    def half(layer, seq):
        return w.at[layer, seq, pl.ds(2 * b, 2)]

    def column(r, other=False):
        side = 1 - xx if other else xx
        return ((z + zs - r) % zs) * 2 + side

    order = [1, zs - 1] + list(range(2, zs - 1))
    wz, wx, wy, wc = {}, {}, {}, {}

    def send_x(layer, r):
        c = quarter(layer, column(r))
        wx[layer, r] = launch(copy(c, c, wx_s.at[layer, r], wx_r.at[layer, r], to(xp, b)))

    def send_y(layer, r, other):
        c = quarter(layer, column(r, other))
        at = r + (zs if other else 0)
        wy[layer, at] = launch(copy(c, c, wy_s.at[layer, at], wy_r.at[layer, at], over_y))

    def send_core(layer, r, other):
        c = half(layer, column(r, other))
        at = r + (zs if other else 0)
        wc[layer, at] = launch(copy(c, c, wc_s.at[layer, at], wc_r.at[layer, at], to(s, 1 - b)))

    def weights_start(layer):
        for r in range(1, zs):
            c = quarter(layer, s)
            wz[layer, r] = launch(
                copy(c, c, wz_s.at[layer, r - 1], wz_r.at[layer, r - 1], to(((z + r) % zs) * 2 + xx, b))
            )
        send_x(layer, 0)

    def weights_z(layer):
        for r in order:
            wz[layer, r].wait_recv()
            send_x(layer, r)
            send_y(layer, r, False)

    def weights_x(layer):
        for r in [0] + order:
            wx[layer, r].wait_recv()
            send_y(layer, r, True)

    def weights_y(layer):
        for r in order:
            wy[layer, r].wait_recv()
            send_core(layer, r, False)
        for r in [0] + order:
            wy[layer, zs + r].wait_recv()
            send_core(layer, r, True)

    def weights_core(layer):
        for at in range(1, 2 * zs):
            wc[layer, at].wait_recv()

    def tap_of(layer, tap):
        return w[layer, :, tap].reshape(count * rows, w.shape[-1])

    weights_start(0)
    start_halo(0)
    weights_start(1)
    start_halo(1)

    def own_gelu(t):
        v = x_ref[pl.ds(t, 16), :]
        xf[pl.ds(HALO + t, 16), :] = v
        v = v.astype(f32)
        cdf = cdf_of(v)
        h1[pl.ds(HALO + t, 16), :] = (v * cdf).astype(bf)
        s1[pl.ds(t, 16), :] = slope_of(v, cdf)

    over_rows(0, n, 16, own_gelu)
    cf[pl.ds(MARGIN_ONE, n), :] = c_ref[...]

    def blank(ref, first, height):
        ref[pl.ds(first, height), :] = jnp.zeros((height, ref.shape[1]), ref.dtype)

    blank(xf, 0, HALO - NEAR)
    blank(xf, HALO + n + NEAR, HALO - NEAR)
    blank(cf, 0, MARGIN_ONE - NEAR_TOP)
    blank(cf, MARGIN_ONE + n + NEAR_TOP, MARGIN_ONE - NEAR_TOP)
    weights_z(0)
    weights_x(0)
    weights_y(0)

    for sends, receives, pair, xdst, cdst in halo_copies:
        @pl.when(receives)
        def _():
            pair[0].wait_recv()

        @pl.when(jnp.logical_not(receives))
        def _():
            blank(xf, xdst, NEAR)

    def halo_gelu(t):
        v = xf[pl.ds(t, 16), :].astype(f32)
        h1[pl.ds(t, 16), :] = (v * cdf_of(v)).astype(bf)

    over_rows(0, HALO, 16, halo_gelu)
    over_rows(HALO + n, 2 * HALO + n, 16, halo_gelu)
    weights_z(1)
    weights_core(0)

    def convolve(h, layer, total):
        def body(t):
            tile = h[pl.ds(t, TILE), :]
            a0[pl.ds(t, TILE), :] = nn(tile, tap_of(layer, 0))
            a1[pl.ds(t, TILE), :] = nn(tile, tap_of(layer, 1))
            a2[pl.ds(t, TILE), :] = nn(tile, tap_of(layer, 2))

        over_rows(0, total, TILE, body)

    mid = n + 2 * MARGIN_MID
    one = n + 2 * MARGIN_ONE

    convolve(h1, 0, n + 2 * HALO)
    off = HALO - MARGIN_MID
    d = FIRST_SPACING
    for t in range(0, mid, 64):
        u1[pl.ds(t, 64), :] = (
            a0[pl.ds(t + off - d, 64), :] + a1[pl.ds(t + off, 64), :] + a2[pl.ds(t + off + d, 64), :]
        )

    def gelu_u1(t):
        v = u1[pl.ds(t, 32), :]
        v1[pl.ds(t, 32), :] = (v * cdf_of(v)).astype(bf)

    over_rows(0, mid, 32, gelu_u1)
    weights_x(1)

    weights_y(1)

    def mix_body(t):
        out = xf[pl.ds(t + off, TILE), :].astype(f32) + nt(v1[pl.ds(t, TILE), :], tap_of(0, 3))
        x2[pl.ds(t, TILE), :] = out.astype(bf)

    over_rows(0, mid, TILE, mix_body)

    def both_x2(t):
        v = x2[pl.ds(t, 16), :].astype(f32)
        cdf = cdf_of(v)
        h2[pl.ds(t, 16), :] = (v * cdf).astype(bf)
        s2[pl.ds(t, 16), :] = slope_of(v, cdf)

    over_rows(0, mid, 16, both_x2)

    @pl.when(s == 0)
    def _():
        h2[pl.ds(0, MARGIN_MID), :] = jnp.zeros((MARGIN_MID, h2.shape[1]), bf)

    @pl.when(s == count - 1)
    def _():
        h2[pl.ds(MARGIN_MID + n, MARGIN_MID), :] = jnp.zeros((MARGIN_MID, h2.shape[1]), bf)

    weights_core(1)
    convolve(h2, 1, mid)
    off2 = MARGIN_MID
    d = SECOND_SPACING
    for t in range(0, n, 64):
        u2[pl.ds(t, 64), :] = (
            a0[pl.ds(t + off2 - d, 64), :] + a1[pl.ds(t + off2, 64), :] + a2[pl.ds(t + off2 + d, 64), :]
        )

    def inner_two(t):
        v = u2[pl.ds(t, 64), :]
        out = nn(cf[pl.ds(t + MARGIN_ONE, 64), :], tap_of(1, 3)) * slope_of(v, cdf_of(v))
        db[pl.ds(t, 64), :] = out.astype(bf)
        du[pl.ds(t + HALO, 64), :] = out

    over_rows(0, n, 64, inner_two)
    start_halo(2)
    for sends, receives, pair, xdst, cdst in halo_copies:
        @pl.when(receives)
        def _():
            pair[1].wait_recv()

        @pl.when(jnp.logical_not(receives))
        def _():
            blank(cf, cdst, NEAR_TOP)

    blank(du, 0, HALO - NEAR)
    blank(du, HALO + n + NEAR, HALO - NEAR)
    for at, (sends, receives, pair, xdst, cdst) in enumerate(halo_copies):
        @pl.when(receives)
        def _():
            pair[2].wait_recv()
            du[pl.ds(xdst, NEAR), :] = dh[at].astype(f32)

        @pl.when(jnp.logical_not(receives))
        def _():
            blank(du, xdst, NEAR)

    width = du.shape[1]

    def side_by_side(total, off, d):
        for t in range(0, total, 64):
            for k, at in enumerate((off + d, off, off - d)):
                cat[pl.ds(t, 64), pl.ds(k * width, width)] = du[pl.ds(t + at, 64), :].astype(bf)

    def partial(slot, h, first, offset):
        for k in range(3):
            p = tn(h[pl.ds(first, n), :], cat[pl.ds(offset, n), pl.ds(k * width, width)]).astype(bf)
            for i in range(2 * count):
                pb[slot, i % 2, (i // 2) % 2, i // 4, k] = p[i * sub : (i + 1) * sub]

    def reduce_core(slot):
        return launch(copy(pb.at[slot, 1 - b], r1.at[slot], p1s.at[slot], p1r.at[slot], to(s, 1 - b)))

    def reduce_x(slot, c):
        c.wait_recv()

        def add(side):
            for i in range(zs):
                sm[slot, side, i] = (
                    pb[slot, b, side, i].astype(f32) + r1[slot, side, i].astype(f32)
                ).astype(bf)

        add(1 - xx)
        c = launch(copy(sm.at[slot, 1 - xx], r2.at[slot], p2s.at[slot], p2r.at[slot], to(xp, b)))
        add(xx)
        return c

    def reduce_z(slot, c):
        c.wait_recv()
        for i in range(zs):
            q[slot, i] = (sm[slot, xx, i].astype(f32) + r2[slot, i].astype(f32)).astype(bf)
        return [
            launch(
                copy(
                    q.at[slot, (z + r) % zs], r3.at[slot, r - 1], p3s.at[slot, r - 1], p3r.at[slot, r - 1],
                    to(((z + r) % zs) * 2 + xx, b),
                )
            )
            for r in range(1, zs)
        ]

    def reduce_end(slot, cs):
        total = q[slot, z].astype(f32)
        for r, c in enumerate(cs):
            c.wait_recv()
            total += r3[slot, r].astype(f32)
        return (total * factor).astype(bf)

    side_by_side(one, HALO - MARGIN_ONE, SECOND_SPACING)
    partial(0, h2, MARGIN_MID, MARGIN_ONE)
    step_two = reduce_core(0)

    def back_of(t, layer, tile):
        out = nt(cat[pl.ds(t, tile), pl.ds(0, width)], tap_of(layer, 0))
        out += nt(cat[pl.ds(t, tile), pl.ds(width, width)], tap_of(layer, 1))
        return out + nt(cat[pl.ds(t, tile), pl.ds(2 * width, width)], tap_of(layer, 2))

    def grad_two(t):
        out = cf[pl.ds(t, 64), :].astype(f32) + back_of(t, 1, 64) * s2[pl.ds(t, 64), :]
        g1[pl.ds(t, 64), :] = out.astype(bf)

    over_rows(0, one, 64, grad_two)

    @pl.when(s == 0)
    def _():
        g1[pl.ds(0, MARGIN_ONE), :] = jnp.zeros((MARGIN_ONE, g1.shape[1]), bf)

    @pl.when(s == count - 1)
    def _():
        g1[pl.ds(MARGIN_ONE + n, MARGIN_ONE), :] = jnp.zeros((MARGIN_ONE, g1.shape[1]), bf)

    step_two = reduce_x(0, step_two)

    def inner_one(t):
        v = u1[pl.ds(t, 64), :]
        du[pl.ds(t, 64), :] = nn(g1[pl.ds(t, 64), :], tap_of(0, 3)) * slope_of(v, cdf_of(v))

    over_rows(0, one, 64, inner_one)
    side_by_side(n, MARGIN_ONE, FIRST_SPACING)
    partial(1, h1, HALO, 0)
    step_one = reduce_core(1)
    step_two = reduce_z(0, step_two)
    step_one = reduce_x(1, step_one)

    def grad_one(t):
        out = g1[pl.ds(t + MARGIN_ONE, 64), :].astype(f32) + back_of(t, 0, 64) * s1[pl.ds(t, 64), :]
        gin_ref[pl.ds(t, 64), :] = out.astype(bf)

    over_rows(0, n, 64, grad_one)

    gb[b, xx, z] = reduce_end(0, step_two)
    own = gb.at[b, xx, z]
    along_z = [
        launch(copy(own, own, gzs.at[r - 1], gzr.at[r - 1], to(((z + r) % zs) * 2 + xx, b)))
        for r in range(1, zs)
    ]
    step_one = reduce_z(1, step_one)
    for c in along_z:
        c.wait_recv()
    whole = gb.at[b, xx]
    along_x = launch(copy(whole, whole, gxs, gxr, to(xp, b)))
    first_ref[...] = reduce_end(1, step_one)
    along_x.wait_recv()
    whole = gb.at[b]
    launch(copy(whole, whole, gcs, gcr, to(s, 1 - b))).wait_recv()
    for i in range(2 * count):
        for k in range(3):
            second_ref[k, pl.ds(i * sub, sub), :] = gb[i % 2, (i // 2) % 2, i // 4, k]

    for c in pending:
        c.wait_send()
    for sends, receives, pair, xdst, cdst in halo_copies:
        @pl.when(sends)
        def _():
            pair[0].wait_send()
            pair[1].wait_send()
            pair[2].wait_send()


def fused(count, batch, inputs, cotangent, kernel_one, mix_one, kernel_two, mix_two):
    n, channels = inputs.shape[1:]
    _, rows, hid = kernel_one.shape
    sub = rows // 2
    zs = count // 2
    bf, f32 = jnp.bfloat16, jnp.float32
    mid, one, frame = n + 2 * MARGIN_MID, n + 2 * MARGIN_ONE, n + 2 * HALO
    vm = pltpu.VMEM
    dma = pltpu.SemaphoreType.DMA
    sems = []
    for shape in ((2, zs - 1), (2, zs), (2, 2 * zs), (4,), (2,), (2,), (2, zs - 1), (zs - 1,)):
        sems += [dma(shape), dma(shape)]
    sems += [dma, dma, dma, dma]
    sems += [dma((2, 2 * zs)), dma((2, 2 * zs)), dma((2,)), dma((2,))]
    grads = (3, sub, hid)
    spec = pl.BlockSpec(memory_space=pltpu.VMEM)
    gin, first, second = pl.pallas_call(
        functools.partial(fused_kernel, n, zs, float(n * count * batch) ** (-0.5)),
        out_shape=(
            jax.ShapeDtypeStruct((n, channels), bf),
            jax.ShapeDtypeStruct(grads, bf),
            jax.ShapeDtypeStruct((3, channels, hid), bf),
        ),
        in_specs=[spec] * 6,
        out_specs=(spec,) * 3,
        scratch_shapes=[
            vm((2, count, 4, rows, hid), bf),
            vm((frame, channels), bf),
            vm((one, channels), bf),
            vm((frame, channels), bf),
            vm((n, channels), f32),
            vm((frame, hid), f32),
            vm((frame, hid), f32),
            vm((frame, hid), f32),
            vm((mid, hid), f32),
            vm((mid, hid), bf),
            vm((mid, channels), bf),
            vm((mid, channels), bf),
            vm((one, channels), f32),
            vm((n, hid), f32),
            vm((frame, hid), f32),
            vm((one, 3 * hid), bf),
            vm((one, channels), bf),
            vm((2, 2, 2, zs) + grads, bf),
            vm((2, 2, zs) + grads, bf),
            vm((2, 2, zs) + grads, bf),
            vm((2, zs) + grads, bf),
            vm((2, zs) + grads, bf),
            vm((2, zs - 1) + grads, bf),
            vm((2, 2, zs) + grads, bf),
            vm((n, hid), bf),
            vm((2, NEAR, hid), bf),
        ]
        + sems,
        compiler_params=pltpu.CompilerParams(
            collective_id=0, has_side_effects=True, vmem_limit_bytes=52 * 2**20
        ),
    )(inputs[0], cotangent[0], kernel_one, mix_one, kernel_two, mix_two)
    return (gin[None], first, second)


def body(groups, count, batch, inputs, *rest):
    n, rows = inputs.shape[1], rest[1].shape[1]
    fits = n >= HALO and n % TILE == 0 and rows % 32 == 0
    if fits and count % 2 == 0 and count >= 6 and batch == 2 and groups == 2:
        return fused(count, batch, inputs, *rest)
    return shards(inputs, *rest)


def solution(mesh):
    placed = (
        P(("groups", "batch"), "seq", None),
        P(("groups", "batch"), "seq", None),
        P(None, "seq", None),
        P(None, "seq"),
        P(None, "seq", None),
        P(None, "seq"),
    )
    return jax.shard_map(
        functools.partial(body, mesh.shape["groups"], mesh.shape["seq"], mesh.shape["batch"]),
        mesh=mesh,
        in_specs=placed,
        out_specs=(
            P(("groups", "batch"), "seq", None),
            P("groups", ("seq", "batch"), None),
            P("groups", None, None),
        ),
        check_vma=False,
    )
```

```python
import functools
import math

import jax
import jax.numpy as jnp
from jax import lax
from jax.experimental import pallas as pl
from jax.experimental.pallas import tpu as pltpu
from jax.sharding import PartitionSpec as P

FIRST_SPACING = 38
SECOND_SPACING = 58


def padded_2(cells, sides, width):
    for axis, dim in sides:
        count = lax.axis_size(axis)
        ends = count - 1
        head = lax.slice_in_dim(cells, 0, width, axis=dim)
        tail = lax.slice_in_dim(cells, cells.shape[dim] - width, cells.shape[dim], axis=dim)
        cells = jnp.concatenate(
            [
                lax.ppermute(tail, axis, [(i, (i + 1) % count) for i in range(ends)]),
                cells,
                lax.ppermute(head, axis, [((i + 1) % count, i) for i in range(ends)]),
            ],
            axis=dim,
        )
    return cells


def gelu_exact(v):
    return 0.5 * v * (1.0 + jax.scipy.special.erf(v / math.sqrt(2.0)))


def gelu_slope(v):
    cdf = 0.5 * (1.0 + jax.scipy.special.erf(v / math.sqrt(2.0)))
    return cdf + v * jnp.exp(-0.5 * v * v) / math.sqrt(2.0 * math.pi)


def mat_nn(left, right):
    return jnp.dot(left, right, preferred_element_type=jnp.float32)


def mat_nt(left, right):
    return lax.dot_general(
        left, right, (((1,), (1,)), ((), ())), preferred_element_type=jnp.float32
    )


def mat_tn(left, right):
    return lax.dot_general(
        left, right, (((0,), (0,)), ((), ())), preferred_element_type=jnp.float32
    )


def inner_convolved(before, hidden, after, kernel):
    return mat_nn(before, kernel[0]) + mat_nn(hidden, kernel[1]) + mat_nn(after, kernel[2])


def block_back(stream, hidden, grad_inner, above, below, kernel, grad_out):
    partial_value = jnp.stack(
        [mat_tn(hidden, above), mat_tn(hidden, grad_inner), mat_tn(hidden, below)]
    )
    back = mat_nt(grad_inner, kernel[1]) + mat_nt(above, kernel[0]) + mat_nt(below, kernel[2])
    grad_in = (grad_out.astype(jnp.float32) + back * gelu_slope(stream.astype(jnp.float32))).astype(
        jnp.bfloat16
    )
    return (grad_in, partial_value)


def shards(inputs, cotangent, kernel_one, mix_one, kernel_two, mix_two):
    stream = inputs[0]
    grad_top = cotangent[0]
    length = stream.shape[0]
    first_spacing_offset = FIRST_SPACING
    second_spacing_offset = SECOND_SPACING
    kern_a, mixer_a, kern_b, mixer_b = (
        lax.all_gather(kernel_one, "seq", axis=1, tiled=True),
        lax.all_gather(mix_one, "seq", axis=1, tiled=True),
        lax.all_gather(kernel_two, "seq", axis=1, tiled=True),
        lax.all_gather(mix_two, "seq", axis=1, tiled=True),
    )
    hidden_one = gelu_exact(stream.astype(jnp.float32)).astype(jnp.bfloat16)
    padded = padded_2(hidden_one, (("seq", 0),), first_spacing_offset)
    inner_one = inner_convolved(
        padded[:length], hidden_one, padded[2 * first_spacing_offset :], kern_a
    )
    active_one = gelu_exact(inner_one).astype(jnp.bfloat16)
    middle = (stream.astype(jnp.float32) + mat_nn(active_one, mixer_a)).astype(jnp.bfloat16)
    hidden_two = gelu_exact(middle.astype(jnp.float32)).astype(jnp.bfloat16)
    padded_two = padded_2(hidden_two, (("seq", 0),), second_spacing_offset)
    inner_two = inner_convolved(
        padded_two[:length], hidden_two, padded_two[2 * second_spacing_offset :], kern_b
    )
    grad_inner_two = (mat_nt(grad_top, mixer_b) * gelu_slope(inner_two)).astype(jnp.bfloat16)
    grad_pad_two = padded_2(grad_inner_two, (("seq", 0),), second_spacing_offset)
    grad_mid, partial_two = block_back(
        middle,
        hidden_two,
        grad_inner_two,
        grad_pad_two[2 * second_spacing_offset :],
        grad_pad_two[:length],
        kern_b,
        grad_top,
    )
    factor = float(length * lax.axis_size("seq") * lax.axis_size("batch")) ** (-0.5)
    share_two = lax.psum_scatter(partial_two, ("seq", "batch"), scatter_dimension=1, tiled=True)
    result_two = lax.all_gather(
        (share_two * factor).astype(jnp.bfloat16), ("seq", "batch"), axis=1, tiled=True
    )
    grad_inner_one = (mat_nt(grad_mid, mixer_a) * gelu_slope(inner_one)).astype(jnp.bfloat16)
    padded_gradient_rows = padded_2(grad_inner_one, (("seq", 0),), first_spacing_offset)
    grad_in, partial_one = block_back(
        stream,
        hidden_one,
        grad_inner_one,
        padded_gradient_rows[2 * first_spacing_offset :],
        padded_gradient_rows[:length],
        kern_a,
        grad_mid,
    )
    share_one = lax.psum_scatter(partial_one, ("seq", "batch"), scatter_dimension=1, tiled=True)
    return (grad_in[None], (share_one * factor).astype(jnp.bfloat16), result_two)


HALO, MARGIN_MID, MARGIN_ONE = 128, 64, 64
NEAR = 96
NEAR_TOP = 48
TILE = 128


def nn(left, right):
    return jnp.dot(left, right, preferred_element_type=jnp.float32)


def nt(left, right):
    return lax.dot_general(
        left, right, (((1,), (1,)), ((), ())), preferred_element_type=jnp.float32
    )


def tn(left, right):
    return lax.dot_general(
        left, right, (((0,), (0,)), ((), ())), preferred_element_type=jnp.float32
    )


def cdf_of(v):
    return 0.5 + 0.5 * lax.erf(v * (1.0 / math.sqrt(2.0)))


def slope_of(v, cdf):
    return cdf + v * jnp.exp(-0.5 * v * v) * (1.0 / math.sqrt(2.0 * math.pi))


def over_rows(start, stop, tile, body):
    def step(i, carry):
        body(pl.multiple_of(start + i * tile, math.gcd(start, tile) if start else tile))
        return carry

    lax.fori_loop(0, (stop - start) // tile, step, 0)


def fused_kernel(
    n, zs, factor,
    x_ref, c_ref, k1_ref, m1_ref, k2_ref, m2_ref,
    gin_ref, first_ref, second_ref,
    w, xf, cf, h1, s1, a0, a1, a2, u1, v1, x2, h2, s2, u2, du, cat, g1,
    pb, r1, sm, r2, q, r3, gb, db, dh,
    wz_s, wz_r, wx_s, wx_r, wc_s, wc_r, hs, hr, p1s, p1r, p2s, p2r, p3s, p3r,
    gzs, gzr, gxs, gxr, gcs, gcr, wy_s, wy_r, ds, dr, ls,
):
    bf, f32 = jnp.bfloat16, jnp.float32
    s = lax.axis_index("seq")
    b = lax.axis_index("batch")
    g = lax.axis_index("groups")
    count = 2 * zs
    z, xx = s // 2, s % 2
    xp = s + 1 - 2 * xx
    rows = k1_ref.shape[1]
    sub = rows // 2

    def to(seq, batch):
        return {"seq": seq, "batch": batch}

    over_y = {"groups": 1 - g}

    def copy(src, dst, send, recv, target):
        return pltpu.make_async_remote_copy(
            src_ref=src, dst_ref=dst, send_sem=send, recv_sem=recv,
            device_id=target, device_id_type=pl.DeviceIdType.MESH,
        )

    x_own = pltpu.make_async_copy(x_ref, xf.at[pl.ds(HALO, n)], ls.at[0])
    c_own = pltpu.make_async_copy(c_ref, cf.at[pl.ds(MARGIN_ONE, n)], ls.at[1])
    x_own.start()
    c_own.start()
    barrier = pltpu.get_barrier_semaphore()
    away = sorted({1, count - 1} | {2 * r for r in range(1, zs)})
    for d in away:
        pl.semaphore_signal(barrier, inc=1, device_id=to((s + d) % count, b), device_id_type=pl.DeviceIdType.MESH)
    pl.semaphore_signal(barrier, inc=1, device_id=to(s, 1 - b), device_id_type=pl.DeviceIdType.MESH)

    pl.semaphore_signal(barrier, inc=1, device_id=over_y, device_id_type=pl.DeviceIdType.MESH)

    eye = (
        lax.broadcasted_iota(jnp.int32, (rows, rows), 0) == lax.broadcasted_iota(jnp.int32, (rows, rows), 1)
    ).astype(f32).astype(bf)
    for layer, (k_ref, m_ref) in enumerate(((k1_ref, m1_ref), (k2_ref, m2_ref))):
        for tap in range(3):
            w[layer, s, tap] = k_ref[tap]
        w[layer, s, 3] = nt(eye, m_ref[...]).astype(bf)
    pl.semaphore_wait(barrier, len(away) + 2)

    pending = []

    def launch(c):
        c.start()
        pending.append(c)
        return c

    halos = (
        (s < count - 1, s > 0, (s + 1) % count, 0),
        (s > 0, s < count - 1, (s + count - 1) % count, 1),
    )

    def edge(which, height, near):
        return (n - near, height - near) if which == 0 else (0, height + n)

    halo_copies = []
    for sends, receives, target, at in halos:
        xsrc, xdst = edge(at, HALO, NEAR)
        csrc, cdst = edge(at, MARGIN_ONE, NEAR_TOP)
        pair = (
            copy(x_ref.at[pl.ds(xsrc, NEAR)], xf.at[pl.ds(xdst, NEAR)], hs.at[2 * at], hr.at[2 * at], to(target, b)),
            copy(c_ref.at[pl.ds(csrc, NEAR_TOP)], cf.at[pl.ds(cdst, NEAR_TOP)], hs.at[2 * at + 1], hr.at[2 * at + 1], to(target, b)),
            copy(db.at[pl.ds(xsrc, NEAR)], dh.at[at], ds.at[at], dr.at[at], to(target, b)),
        )
        halo_copies.append((sends, receives, pair, xdst, cdst))

    def start_halo(which):
        for sends, receives, pair, xdst, cdst in halo_copies:
            @pl.when(sends)
            def _():
                pair[which].start()

    def quarter(layer, seq):
        return w.at[layer, seq, 2 * b + g]

    def half(layer, seq):
        return w.at[layer, seq, pl.ds(2 * b, 2)]

    def column(r, other=False):
        side = 1 - xx if other else xx
        return ((z + zs - r) % zs) * 2 + side

    order = [1, zs - 1] + list(range(2, zs - 1))
    wz, wx, wy, wc = {}, {}, {}, {}

    def send_x(layer, r):
        c = quarter(layer, column(r))
        wx[layer, r] = launch(copy(c, c, wx_s.at[layer, r], wx_r.at[layer, r], to(xp, b)))

    def send_y(layer, r, other):
        c = quarter(layer, column(r, other))
        at = r + (zs if other else 0)
        wy[layer, at] = launch(copy(c, c, wy_s.at[layer, at], wy_r.at[layer, at], over_y))

    def send_core(layer, r, other):
        c = half(layer, column(r, other))
        at = r + (zs if other else 0)
        wc[layer, at] = launch(copy(c, c, wc_s.at[layer, at], wc_r.at[layer, at], to(s, 1 - b)))

    def weights_start(layer):
        for r in range(1, zs):
            c = quarter(layer, s)
            wz[layer, r] = launch(
                copy(c, c, wz_s.at[layer, r - 1], wz_r.at[layer, r - 1], to(((z + r) % zs) * 2 + xx, b))
            )
        send_x(layer, 0)

    def weights_z(layer):
        for r in order:
            wz[layer, r].wait_recv()
            send_x(layer, r)
            send_y(layer, r, False)

    def weights_x(layer):
        for r in [0] + order:
            wx[layer, r].wait_recv()
            send_y(layer, r, True)

    def weights_y(layer):
        for r in order:
            wy[layer, r].wait_recv()
            send_core(layer, r, False)
        for r in [0] + order:
            wy[layer, zs + r].wait_recv()
            send_core(layer, r, True)

    def weights_core(layer):
        for at in range(1, 2 * zs):
            wc[layer, at].wait_recv()

    def tap_of(layer, tap):
        return w[layer, :, tap].reshape(count * rows, w.shape[-1])

    weights_start(0)
    start_halo(0)
    start_halo(1)

    def own_gelu(t):
        v = xf[pl.ds(HALO + t, 16), :].astype(f32)
        cdf = cdf_of(v)
        h1[pl.ds(HALO + t, 16), :] = (v * cdf).astype(bf)
        s1[pl.ds(t, 16), :] = slope_of(v, cdf)

    x_own.wait()
    over_rows(0, n, 16, own_gelu)
    c_own.wait()

    def blank(ref, first, height):
        ref[pl.ds(first, height), :] = jnp.zeros((height, ref.shape[1]), ref.dtype)

    blank(xf, 0, HALO - NEAR)
    blank(xf, HALO + n + NEAR, HALO - NEAR)
    blank(cf, 0, MARGIN_ONE - NEAR_TOP)
    blank(cf, MARGIN_ONE + n + NEAR_TOP, MARGIN_ONE - NEAR_TOP)
    weights_z(0)
    weights_start(1)
    weights_x(0)
    weights_y(0)

    for sends, receives, pair, xdst, cdst in halo_copies:
        @pl.when(receives)
        def _():
            pair[0].wait_recv()

        @pl.when(jnp.logical_not(receives))
        def _():
            blank(xf, xdst, NEAR)

    def halo_gelu(t):
        v = xf[pl.ds(t, 16), :].astype(f32)
        h1[pl.ds(t, 16), :] = (v * cdf_of(v)).astype(bf)

    over_rows(0, HALO, 16, halo_gelu)
    over_rows(HALO + n, 2 * HALO + n, 16, halo_gelu)
    weights_z(1)
    weights_core(0)

    def convolve(h, layer, total):
        def body(t):
            tile = h[pl.ds(t, TILE), :]
            a0[pl.ds(t, TILE), :] = nn(tile, tap_of(layer, 0))
            a1[pl.ds(t, TILE), :] = nn(tile, tap_of(layer, 1))
            a2[pl.ds(t, TILE), :] = nn(tile, tap_of(layer, 2))

        over_rows(0, total, TILE, body)

    mid = n + 2 * MARGIN_MID
    one = n + 2 * MARGIN_ONE

    convolve(h1, 0, n + 2 * HALO)
    off = HALO - MARGIN_MID
    d = FIRST_SPACING
    for t in range(0, mid, 64):
        u1[pl.ds(t, 64), :] = (
            a0[pl.ds(t + off - d, 64), :] + a1[pl.ds(t + off, 64), :] + a2[pl.ds(t + off + d, 64), :]
        )

    def gelu_u1(t):
        v = u1[pl.ds(t, 32), :]
        v1[pl.ds(t, 32), :] = (v * cdf_of(v)).astype(bf)

    over_rows(0, mid, 32, gelu_u1)
    weights_x(1)

    weights_y(1)

    def mix_body(t):
        out = xf[pl.ds(t + off, TILE), :].astype(f32) + nt(v1[pl.ds(t, TILE), :], tap_of(0, 3))
        x2[pl.ds(t, TILE), :] = out.astype(bf)

    over_rows(0, mid, TILE, mix_body)

    def both_x2(t):
        v = x2[pl.ds(t, 16), :].astype(f32)
        cdf = cdf_of(v)
        h2[pl.ds(t, 16), :] = (v * cdf).astype(bf)
        s2[pl.ds(t, 16), :] = slope_of(v, cdf)

    over_rows(0, mid, 16, both_x2)

    @pl.when(s == 0)
    def _():
        h2[pl.ds(0, MARGIN_MID), :] = jnp.zeros((MARGIN_MID, h2.shape[1]), bf)

    @pl.when(s == count - 1)
    def _():
        h2[pl.ds(MARGIN_MID + n, MARGIN_MID), :] = jnp.zeros((MARGIN_MID, h2.shape[1]), bf)

    weights_core(1)
    convolve(h2, 1, mid)
    off2 = MARGIN_MID
    d = SECOND_SPACING
    for t in range(0, n, 64):
        u2[pl.ds(t, 64), :] = (
            a0[pl.ds(t + off2 - d, 64), :] + a1[pl.ds(t + off2, 64), :] + a2[pl.ds(t + off2 + d, 64), :]
        )

    def inner_two(t):
        v = u2[pl.ds(t, 64), :]
        out = nn(cf[pl.ds(t + MARGIN_ONE, 64), :], tap_of(1, 3)) * slope_of(v, cdf_of(v))
        db[pl.ds(t, 64), :] = out.astype(bf)
        du[pl.ds(t + HALO, 64), :] = out

    over_rows(0, n, 64, inner_two)
    start_halo(2)
    for sends, receives, pair, xdst, cdst in halo_copies:
        @pl.when(receives)
        def _():
            pair[1].wait_recv()

        @pl.when(jnp.logical_not(receives))
        def _():
            blank(cf, cdst, NEAR_TOP)

    blank(du, 0, HALO - NEAR)
    blank(du, HALO + n + NEAR, HALO - NEAR)
    for at, (sends, receives, pair, xdst, cdst) in enumerate(halo_copies):
        @pl.when(receives)
        def _():
            pair[2].wait_recv()
            du[pl.ds(xdst, NEAR), :] = dh[at].astype(f32)

        @pl.when(jnp.logical_not(receives))
        def _():
            blank(du, xdst, NEAR)

    width = du.shape[1]

    def side_by_side(total, off, d):
        for t in range(0, total, 64):
            for k, at in enumerate((off + d, off, off - d)):
                cat[pl.ds(t, 64), pl.ds(k * width, width)] = du[pl.ds(t + at, 64), :].astype(bf)

    def partial(slot, h, first, offset):
        for k in range(3):
            p = tn(h[pl.ds(first, n), :], cat[pl.ds(offset, n), pl.ds(k * width, width)]).astype(bf)
            for i in range(2 * count):
                pb[slot + k, i % 2, (i // 2) % 2, i // 4] = p[i * sub : (i + 1) * sub]
            yield reduce_core(slot + k)

    def reduce_core(slot):
        return launch(copy(pb.at[slot, 1 - b], r1.at[slot], p1s.at[slot], p1r.at[slot], to(s, 1 - b)))

    def reduce_x(slot, c):
        c.wait_recv()

        def add(side):
            for i in range(zs):
                sm[slot, side, i] = (
                    pb[slot, b, side, i].astype(f32) + r1[slot, side, i].astype(f32)
                ).astype(bf)

        add(1 - xx)
        c = launch(copy(sm.at[slot, 1 - xx], r2.at[slot], p2s.at[slot], p2r.at[slot], to(xp, b)))
        add(xx)
        return c

    def reduce_z(slot, c):
        c.wait_recv()
        for i in range(zs):
            q[slot, i] = (sm[slot, xx, i].astype(f32) + r2[slot, i].astype(f32)).astype(bf)
        return [
            launch(
                copy(
                    q.at[slot, (z + r) % zs], r3.at[slot, r - 1], p3s.at[slot, r - 1], p3r.at[slot, r - 1],
                    to(((z + r) % zs) * 2 + xx, b),
                )
            )
            for r in range(1, zs)
        ]

    def reduce_end(slot, cs):
        total = q[slot, z].astype(f32)
        for r, c in enumerate(cs):
            c.wait_recv()
            total += r3[slot, r].astype(f32)
        return (total * factor).astype(bf)

    side_by_side(one, HALO - MARGIN_ONE, SECOND_SPACING)
    step_two = list(partial(0, h2, MARGIN_MID, MARGIN_ONE))

    def back_of(t, layer, tile):
        out = nt(cat[pl.ds(t, tile), pl.ds(0, width)], tap_of(layer, 0))
        out += nt(cat[pl.ds(t, tile), pl.ds(width, width)], tap_of(layer, 1))
        return out + nt(cat[pl.ds(t, tile), pl.ds(2 * width, width)], tap_of(layer, 2))

    def grad_two(t):
        out = cf[pl.ds(t, 64), :].astype(f32) + back_of(t, 1, 64) * s2[pl.ds(t, 64), :]
        g1[pl.ds(t, 64), :] = out.astype(bf)

    over_rows(0, one, 64, grad_two)

    @pl.when(s == 0)
    def _():
        g1[pl.ds(0, MARGIN_ONE), :] = jnp.zeros((MARGIN_ONE, g1.shape[1]), bf)

    @pl.when(s == count - 1)
    def _():
        g1[pl.ds(MARGIN_ONE + n, MARGIN_ONE), :] = jnp.zeros((MARGIN_ONE, g1.shape[1]), bf)

    step_two = [reduce_x(k, step_two[k]) for k in range(3)]

    def inner_one(t):
        v = u1[pl.ds(t, 64), :]
        du[pl.ds(t, 64), :] = nn(g1[pl.ds(t, 64), :], tap_of(0, 3)) * slope_of(v, cdf_of(v))

    over_rows(0, one, 64, inner_one)
    side_by_side(n, MARGIN_ONE, FIRST_SPACING)
    step_one = list(partial(3, h1, HALO, 0))
    step_two = [reduce_z(k, step_two[k]) for k in range(3)]
    step_one = [reduce_x(3 + k, step_one[k]) for k in range(3)]

    def grad_one(t):
        out = g1[pl.ds(t + MARGIN_ONE, 64), :].astype(f32) + back_of(t, 0, 64) * s1[pl.ds(t, 64), :]
        gin_ref[pl.ds(t, 64), :] = out.astype(bf)

    over_rows(0, n, 64, grad_one)

    for k in range(3):
        gb[b, xx, z, k] = reduce_end(k, step_two[k])
    own = gb.at[b, xx, z]
    along_z = [
        launch(copy(own, own, gzs.at[r - 1], gzr.at[r - 1], to(((z + r) % zs) * 2 + xx, b)))
        for r in range(1, zs)
    ]

    def share(r, other, sends, receives, at, target):
        block = gb.at[b, 1 - xx if other else xx, (z + zs - r) % zs]
        return launch(copy(block, block, sends.at[at], receives.at[at], target))

    across = {0: share(0, False, gxs, gxr, 0, to(xp, b))}
    inside = [share(0, False, gcs, gcr, 0, to(s, 1 - b))]
    step_one = [reduce_z(3 + k, step_one[k]) for k in range(3)]
    for r in order:
        along_z[r - 1].wait_recv()
        across[r] = share(r, False, gxs, gxr, r, to(xp, b))
        inside.append(share(r, False, gcs, gcr, r, to(s, 1 - b)))
    for r in [0] + order:
        across[r].wait_recv()
        inside.append(share(r, True, gcs, gcr, zs + r, to(s, 1 - b)))
    for k in range(3):
        first_ref[k] = reduce_end(3 + k, step_one[k])
    for c in inside:
        c.wait_recv()
    for i in range(2 * count):
        for k in range(3):
            second_ref[k, pl.ds(i * sub, sub), :] = gb[i % 2, (i // 2) % 2, i // 4, k]

    for c in pending:
        c.wait_send()
    for sends, receives, pair, xdst, cdst in halo_copies:
        @pl.when(sends)
        def _():
            pair[0].wait_send()
            pair[1].wait_send()
            pair[2].wait_send()


def fused(count, batch, inputs, cotangent, kernel_one, mix_one, kernel_two, mix_two):
    n, channels = inputs.shape[1:]
    _, rows, hid = kernel_one.shape
    sub = rows // 2
    zs = count // 2
    bf, f32 = jnp.bfloat16, jnp.float32
    mid, one, frame = n + 2 * MARGIN_MID, n + 2 * MARGIN_ONE, n + 2 * HALO
    vm = pltpu.VMEM
    dma = pltpu.SemaphoreType.DMA
    sems = []
    for shape in ((2, zs - 1), (2, zs), (2, 2 * zs), (4,), (6,), (6,), (6, zs - 1), (zs - 1,)):
        sems += [dma(shape), dma(shape)]
    sems += [dma((zs,)), dma((zs,)), dma((2 * zs,)), dma((2 * zs,))]
    sems += [dma((2, 2 * zs)), dma((2, 2 * zs)), dma((2,)), dma((2,)), dma((2,))]
    grads = (3, sub, hid)
    spec = pl.BlockSpec(memory_space=pltpu.VMEM)
    gin, first, second = pl.pallas_call(
        functools.partial(fused_kernel, n, zs, float(n * count * batch) ** (-0.5)),
        out_shape=(
            jax.ShapeDtypeStruct((n, channels), bf),
            jax.ShapeDtypeStruct(grads, bf),
            jax.ShapeDtypeStruct((3, channels, hid), bf),
        ),
        in_specs=[pl.BlockSpec(memory_space=pl.ANY)] * 2 + [spec] * 4,
        out_specs=(spec,) * 3,
        scratch_shapes=[
            vm((2, count, 4, rows, hid), bf),
            vm((frame, channels), bf),
            vm((one, channels), bf),
            vm((frame, channels), bf),
            vm((n, channels), f32),
            vm((frame, hid), f32),
            vm((frame, hid), f32),
            vm((frame, hid), f32),
            vm((mid, hid), f32),
            vm((mid, hid), bf),
            vm((mid, channels), bf),
            vm((mid, channels), bf),
            vm((one, channels), f32),
            vm((n, hid), f32),
            vm((frame, hid), f32),
            vm((one, 3 * hid), bf),
            vm((one, channels), bf),
            vm((6, 2, 2, zs) + grads[1:], bf),
            vm((6, 2, zs) + grads[1:], bf),
            vm((6, 2, zs) + grads[1:], bf),
            vm((6, zs) + grads[1:], bf),
            vm((6, zs) + grads[1:], bf),
            vm((6, zs - 1) + grads[1:], bf),
            vm((2, 2, zs) + grads, bf),
            vm((n, hid), bf),
            vm((2, NEAR, hid), bf),
        ]
        + sems,
        compiler_params=pltpu.CompilerParams(
            collective_id=0, has_side_effects=True, vmem_limit_bytes=52 * 2**20
        ),
    )(inputs[0], cotangent[0], kernel_one, mix_one, kernel_two, mix_two)
    return (gin[None], first, second)


def body(groups, count, batch, inputs, *rest):
    n, rows = inputs.shape[1], rest[1].shape[1]
    fits = n >= HALO and n % TILE == 0 and rows % 32 == 0
    if fits and count % 2 == 0 and count >= 6 and batch == 2 and groups == 2:
        return fused(count, batch, inputs, *rest)
    return shards(inputs, *rest)


def solution(mesh):
    placed = (
        P(("groups", "batch"), "seq", None),
        P(("groups", "batch"), "seq", None),
        P(None, "seq", None),
        P(None, "seq"),
        P(None, "seq", None),
        P(None, "seq"),
    )
    return jax.shard_map(
        functools.partial(body, mesh.shape["groups"], mesh.shape["seq"], mesh.shape["batch"]),
        mesh=mesh,
        in_specs=placed,
        out_specs=(
            P(("groups", "batch"), "seq", None),
            P("groups", ("seq", "batch"), None),
            P("groups", None, None),
        ),
        check_vma=False,
    )
```
